32 devices in a mesh: energy: 8 (over z, y), momentum: 4 (over x, core).
Axes of the slice: x: 2, y: 2, z: 4, core: 2. Of those that a mesh axis runs over, the one named last changes fastest.
Arguments:
- device_hamiltonian: float32 [4, 2, 256, 256], P('momentum'), may hold values from -3 to 1, as said below
- lead_hamiltonian: float32 [4, 2, 256, 256], P('momentum'), may hold values from -3 to 1, as said below
- lead_coupling: float32 [4, 2, 256, 256], P('momentum'), may hold values from -0.28 to 0.28
- pair_atoms: int32 [2, 128], replicated, may hold values from 0 to 20, as said below
- phonon_shift: int32 [4], replicated, may hold values from 1 to 7
- occupation: float32 [4], replicated, may hold values from 0.2 to 1.5
- phonon_coupling: float32 [4, 128], replicated, may hold values from 0.1 to 0.4
Outputs:
- green_final: float32 [8, 4, 2, 256, 256], P('energy', 'momentum')
The draws below stay inside these ranges and needn't reach their ends.
Inputs may be any that keep to these rules, and one draw needn't show every extreme that they name: `device_hamiltonian`: each diagonal entry has its real part in [-1, 1] and its imaginary part in [-3, -1.5]; off-diagonal entries lie within 0.21 in magnitude. `lead_hamiltonian`: each diagonal entry has its real part in [-1, 1] and its imaginary part in [-3, -1.5]; off-diagonal entries lie within 0.12 in magnitude. `pair_atoms`: the first 21 pairs join each atom with itself, in order; every other pair joins two different atoms.
All inputs are finite; a program needn't handle non-finite values.
Results may differ from the reference program's by a relative error of at most 0.00011.
Values sent between devices are 32-bit elements; how exact they have to be, the bound alone decides.
A program may use at most 64 MiB of HBM per device.

```python
import math
import jax
import jax.numpy as jnp
from jax import lax

B = 256
ORB = 12
ATOMS = 21
PAIRS = 128
MODES = 4
NEWTON = 2
E_ALL = 8
MOMENTA = 4


def pair_list(key):
    first_key, offset_key = jax.random.split(jax.random.fold_in(key, 37))
    extra_pairs = PAIRS - ATOMS
    first_atoms = jax.random.randint(first_key, (extra_pairs,), 0, ATOMS, dtype=jnp.int32)
    offsets = jax.random.randint(offset_key, (extra_pairs,), 1, ATOMS, dtype=jnp.int32)
    second_atoms = (first_atoms + offsets) % ATOMS
    own_atoms = jnp.arange(ATOMS, dtype=jnp.int32)
    return jnp.stack([jnp.concatenate([own_atoms, first_atoms]), jnp.concatenate([own_atoms, second_atoms])]).astype(jnp.int32)


def neighbour_blocks(key, pairs):
    real_key, imag_key = jax.random.split(jax.random.fold_in(key, 53))
    atom_rows = ATOMS * ORB
    shape = (atom_rows, atom_rows)
    real_part = 0.05 * jnp.clip(jax.random.normal(real_key, shape, jnp.float32), -3.0, 3.0)
    imag_part = 0.025 * jnp.clip(jax.random.normal(imag_key, shape, jnp.float32), -3.0, 3.0)
    occupied = jnp.zeros((ATOMS, ATOMS), jnp.float32).at[pairs[0], pairs[1]].set(1.0)
    spread_mask = jnp.broadcast_to(occupied[:, None, :, None], (ATOMS, ORB, ATOMS, ORB)).reshape(atom_rows, atom_rows)
    spread_mask = spread_mask * (1.0 - jnp.eye(atom_rows, dtype=jnp.float32))
    spare_rows = B - atom_rows
    padding = ((0, spare_rows), (0, spare_rows))
    return (jnp.pad(real_part * spread_mask, padding), jnp.pad(imag_part * spread_mask, padding))


def random_slab(key):
    noise_key, onsite_key, absorb_key = jax.random.split(key, 3)
    shape = (MOMENTA, 2, B, B)
    spread = 0.02 * jnp.clip(jax.random.normal(noise_key, shape, jnp.float32), -6.0, 6.0)
    identity = jnp.eye(B, dtype=jnp.float32)
    onsite = jax.random.uniform(onsite_key, (MOMENTA, B), jnp.float32, -1.0, 1.0)
    absorb = jax.random.uniform(absorb_key, (MOMENTA, B), jnp.float32, 1.5, 3.0)
    real_part = spread[:, 0] * (1.0 - identity) + onsite[:, :, None] * identity
    imag_part = spread[:, 1] * (1.0 - identity) - absorb[:, :, None] * identity
    return jnp.stack([real_part, imag_part], axis=1)


def device_slab(key):
    noise_key, onsite_key, absorb_key, moving_key, damping_key = jax.random.split(jax.random.fold_in(key, 11), 5)
    shape = (MOMENTA, 2, B, B)
    spread = 0.01 * jnp.clip(jax.random.normal(noise_key, shape, jnp.float32), -6.0, 6.0)
    identity = jnp.eye(B, dtype=jnp.float32)
    onsite = jax.random.uniform(onsite_key, (B,), jnp.float32, -0.7, 0.7)[None, :] + jax.random.uniform(moving_key, (MOMENTA, B), jnp.float32, -0.3, 0.3)
    absorb = jax.random.uniform(absorb_key, (B,), jnp.float32, 1.5, 2.7)[None, :] + jax.random.uniform(damping_key, (MOMENTA, B), jnp.float32, 0.0, 0.3)
    neighbour_real, neighbour_imag = neighbour_blocks(key, pair_list(key))
    real_part = spread[:, 0] * (1.0 - identity) + neighbour_real[None] + onsite[:, :, None] * identity
    imag_part = spread[:, 1] * (1.0 - identity) + neighbour_imag[None] - absorb[:, :, None] * identity
    return jnp.stack([real_part, imag_part], axis=1)


def draw_device_hamiltonian(key, part):
    return device_slab(key)


def draw_lead_hamiltonian(key, part):
    return random_slab(jax.random.fold_in(key, 23))


def draw_lead_coupling(key, part):
    shape = (MOMENTA, 2, B, B)
    noise = jax.random.normal(jax.random.fold_in(key, 71), shape, jnp.float32)
    coupling = 0.035 * jnp.clip(noise, -8.0, 8.0)
    return coupling


def draw_pair_atoms(key, part):
    return pair_list(key)


def touch_ends(values, key, least, top_value):
    longest = values.shape.index(max(values.shape))
    spots = []
    for shift in (0, 1):
        where = [jax.random.randint(jax.random.fold_in(key, axis), (), 0, length) for axis, length in enumerate(values.shape)]
        where[longest] = (where[longest] + shift) % values.shape[longest]
        spots.append(tuple(where))
    return values.at[spots[0]].set(least).at[spots[1]].set(top_value)


def setup_inputs(seed: int = 0) -> dict:
    keys = jax.random.split(jax.random.key(seed), 8)
    return {
        "device_hamiltonian": draw_device_hamiltonian(jax.random.fold_in(keys[7], 71), 0),
        "lead_hamiltonian": draw_lead_hamiltonian(jax.random.fold_in(keys[7], 71), 0),
        "lead_coupling": draw_lead_coupling(jax.random.fold_in(keys[7], 71), 0),
        "pair_atoms": draw_pair_atoms(jax.random.fold_in(keys[7], 71), 0),
        "phonon_shift": touch_ends(jax.random.randint(keys[4], (MODES,), 1, E_ALL), jax.random.fold_in(keys[4], 1), 1, E_ALL - 1).astype(jnp.int32),
        "occupation": jnp.clip(jnp.exp(jax.random.uniform(keys[5], (MODES,), jnp.float32, math.log(0.2), math.log(1.5))), 0.2, 1.5),
        "phonon_coupling": jnp.clip(jax.random.uniform(keys[6], (MODES, PAIRS), jnp.float32, 0.1, 0.4), 0.1, 0.4),
    }


HIGHEST_PRECISION = lax.Precision.HIGHEST


def complex_product(left_factor, right_factor):
    left_real = left_factor[..., 0, :, :]
    left_imag = left_factor[..., 1, :, :]
    right_real = right_factor[..., 0, :, :]
    right_imag = right_factor[..., 1, :, :]
    real_part = jnp.matmul(left_real, right_real, precision=HIGHEST_PRECISION) - jnp.matmul(left_imag, right_imag, precision=HIGHEST_PRECISION)
    imag_part = jnp.matmul(left_real, right_imag, precision=HIGHEST_PRECISION) + jnp.matmul(left_imag, right_real, precision=HIGHEST_PRECISION)
    return jnp.stack([real_part, imag_part], axis=-3)


def make_system(energy, hamiltonian):
    identity = jnp.eye(hamiltonian.shape[-1], dtype=jnp.float32)
    real_part = energy[:, None, None, None] * identity - hamiltonian[None, :, 0]
    imag_part = jnp.zeros_like(real_part) - hamiltonian[None, :, 1]
    return jnp.stack([real_part, imag_part], axis=2)


def diagonal_step(system, bare_system):
    diag_real = jnp.diagonal(bare_system[..., 0, :, :], axis1=-2, axis2=-1)
    diag_imag = jnp.diagonal(bare_system[..., 1, :, :], axis1=-2, axis2=-1)
    modulus = diag_real * diag_real + diag_imag * diag_imag
    inverse_real = diag_real / modulus
    inverse_imag = -diag_imag / modulus
    system_real = system[..., 0, :, :]
    system_imag = system[..., 1, :, :]
    column_real = system_real * inverse_real[..., None, :] - system_imag * inverse_imag[..., None, :]
    column_imag = system_real * inverse_imag[..., None, :] + system_imag * inverse_real[..., None, :]
    both_real = inverse_real[..., :, None] * column_real - inverse_imag[..., :, None] * column_imag
    both_imag = inverse_real[..., :, None] * column_imag + inverse_imag[..., :, None] * column_real
    identity = jnp.eye(system.shape[-1], dtype=jnp.float32)
    start_real = 2.0 * identity * inverse_real[..., None, :] - both_real
    start_imag = 2.0 * identity * inverse_imag[..., None, :] - both_imag
    return jnp.stack([start_real, start_imag], axis=-3)


def newton(system, initial, repeats):
    current = initial
    for repeat_index in range(repeats):
        residual = complex_product(system, current)
        current = 2.0 * current - complex_product(current, residual)
    return current


def first_round(energy, device_hamiltonian, lead_hamiltonian, lead_coupling):
    lead_system = make_system(energy, lead_hamiltonian)
    green_lead = newton(lead_system, diagonal_step(lead_system, lead_system), NEWTON)
    contact = complex_product(complex_product(lead_coupling, green_lead), jnp.swapaxes(lead_coupling, -1, -2))
    bare_system = make_system(energy, device_hamiltonian)
    device_system = bare_system - contact
    green_device = newton(device_system, diagonal_step(device_system, bare_system), NEWTON)
    return device_system, green_device


def pair_sums(green_device, pair_atoms):
    atom_rows = ATOMS * ORB
    trimmed = green_device[..., :atom_rows, :atom_rows]
    shaped = trimmed.reshape(trimmed.shape[:3] + (ATOMS, ORB, ATOMS, ORB))
    selected = shaped[:, :, :, pair_atoms[0], :, pair_atoms[1], :]
    summed = jnp.sum(selected, axis=2)
    return jnp.transpose(summed, (1, 2, 3, 4, 0)).reshape(summed.shape[1], 2 * ORB * ORB, summed.shape[0])


def convolve(blocks, phonon_shift, occupation, phonon_coupling):
    energy_count = blocks.shape[0]
    source_index = jnp.arange(energy_count, dtype=jnp.int32)[:, None]
    target_index = jnp.arange(energy_count, dtype=jnp.int32)[None, :]
    flattened = blocks.reshape(energy_count, -1)
    result = jnp.zeros(blocks.shape, jnp.float32)
    for phonon_mode in range(MODES):
        shift_value = phonon_shift[phonon_mode]
        below = (source_index == target_index - shift_value).astype(jnp.float32)
        above = (source_index == target_index + shift_value).astype(jnp.float32)
        kernel = occupation[phonon_mode] * below + (occupation[phonon_mode] + 1.0) * above
        shifted = jnp.dot(kernel.T, flattened, precision=HIGHEST_PRECISION).reshape(blocks.shape)
        result = result + shifted * phonon_coupling[phonon_mode][None, None, :]
    return result


def place_pairs(self_energy, pair_atoms):
    energy_count = self_energy.shape[0]
    values = jnp.transpose(self_energy.reshape(energy_count, 2, ORB, ORB, -1), (4, 0, 1, 2, 3))
    canvas = jnp.zeros((energy_count, 2, ATOMS, ORB, ATOMS, ORB), jnp.float32)
    canvas = canvas.at[:, :, pair_atoms[0], :, pair_atoms[1], :].add(values)
    atom_rows = ATOMS * ORB
    matrix = canvas.reshape(energy_count, 2, atom_rows, atom_rows)
    spare_rows = B - atom_rows
    return jnp.pad(matrix, ((0, 0), (0, 0), (0, spare_rows), (0, spare_rows)))


def reference(device_hamiltonian, lead_hamiltonian, lead_coupling, pair_atoms, phonon_shift, occupation, phonon_coupling):
    energies = -1.0 + 2.0 * (jnp.arange(E_ALL, dtype=jnp.float32) + 0.5) / E_ALL

    def gather_blocks(energy):
        device_system, green_device = first_round(energy[None], device_hamiltonian, lead_hamiltonian, lead_coupling)
        return pair_sums(green_device, pair_atoms)[0]

    averaged = lax.map(gather_blocks, energies) / MOMENTA
    self_energy = convolve(averaged, phonon_shift, occupation, phonon_coupling)

    def second_round(inputs):
        energy, own_energy = inputs
        device_system, green_device = first_round(energy[None], device_hamiltonian, lead_hamiltonian, lead_coupling)
        second_system = device_system - place_pairs(own_energy[None], pair_atoms)[:, None]
        return newton(second_system, green_device, NEWTON)[0]

    return lax.map(second_round, (energies, self_energy))
```

```python
import functools

import jax
import jax.numpy as jnp
from jax import lax
from jax.experimental import pallas as pl
from jax.experimental.pallas import tpu as pltpu
from jax.sharding import PartitionSpec as P

ORB = 12
NEWTON = 2
LANES = 128
F32 = jnp.float32
BF16 = jnp.bfloat16
MESH = pl.DeviceIdType.MESH
VMEM_SPEC = pl.BlockSpec(memory_space=pltpu.VMEM)
SMEM_SPEC = pl.BlockSpec(memory_space=pltpu.SMEM)


def split(value):
    high = value.astype(BF16)
    return high, (value - high.astype(F32)).astype(BF16)


def prepare(matrix):
    real, imag = matrix
    return split(real), split(imag), split(real + imag)


def real_product(left, right, transposed):
    dims = (((1,), (1 if transposed else 0,)), ((), ()))
    dot = functools.partial(lax.dot_general, dimension_numbers=dims, preferred_element_type=F32)
    return dot(left[0], right[0]) + (dot(left[0], right[1]) + dot(left[1], right[0]))


def complex_product(left, right, transposed=False):
    reals = real_product(left[0], right[0], transposed)
    imags = real_product(left[1], right[1], transposed)
    mixed = real_product(left[2], right[2], transposed)
    return reals - imags, mixed - reals - imags


def identity_mask(size):
    rows = lax.broadcasted_iota(jnp.int32, (size, size), 0)
    return rows == lax.broadcasted_iota(jnp.int32, (size, size), 1)


def inverse(real, imag):
    modulus = real * real + imag * imag
    return real / modulus, -imag / modulus


def diagonal_step(system, bare):
    eye = identity_mask(system[0].shape[0])
    masked = [jnp.where(eye, part, 0.0) for part in bare]
    row_real, row_imag = inverse(*[jnp.sum(part, axis=0, keepdims=True) for part in masked])
    col_real, col_imag = inverse(*[jnp.sum(part, axis=1, keepdims=True) for part in masked])
    step_real = system[0] * row_real - system[1] * row_imag
    step_imag = system[0] * row_imag + system[1] * row_real
    both_real = col_real * step_real - col_imag * step_imag
    both_imag = col_real * step_imag + col_imag * step_real
    return (
        jnp.where(eye, 2.0 * row_real, 0.0) - both_real,
        jnp.where(eye, 2.0 * row_imag, 0.0) - both_imag,
    )


def newton(system, current):
    factor = prepare(system)
    for _ in range(NEWTON):
        held = prepare(current)
        residual = complex_product(factor, held)
        change = complex_product(held, prepare(residual))
        current = (2.0 * current[0] - change[0], 2.0 * current[1] - change[1])
    return current


def column_choice(pairs_ref, first, size):
    columns = lax.broadcasted_iota(jnp.int32, (size, pairs_ref.shape[1]), 0)
    starts = ORB * pairs_ref[1:2, :]
    picks = [(columns == starts + (first + j)).astype(F32).astype(BF16) for j in range(2)]
    return jnp.concatenate(picks, axis=1)


def row_choice(pairs_ref, atoms_padded):
    atoms = lax.broadcasted_iota(jnp.int32, (atoms_padded, pairs_ref.shape[1]), 0)
    mask = (atoms == pairs_ref[0:1, :]).astype(F32)
    return jnp.concatenate([mask, mask], axis=1)


def first_kernel(energies, dh_ref, lh_ref, lc_ref, pairs_ref, system_ref, green_ref, blocks_ref, tall):
    size = dh_ref.shape[-1]
    pairs = pairs_ref.shape[1]
    energy = -1.0 + 2.0 * (lax.axis_index("energy").astype(F32) + 0.5) / energies
    eye = identity_mask(size)
    shift = jnp.where(eye, energy, 0.0)
    lead = (shift - lh_ref[0, 0], -lh_ref[0, 1])
    green_lead = newton(lead, diagonal_step(lead, lead))
    coupling = prepare((lc_ref[0, 0], lc_ref[0, 1]))
    contact = complex_product(
        prepare(complex_product(coupling, prepare(green_lead))), coupling, transposed=True
    )
    bare = (shift - dh_ref[0, 0], -dh_ref[0, 1])
    system = (bare[0] - contact[0], bare[1] - contact[1])
    system_ref[0] = system[0]
    system_ref[1] = system[1]
    green = newton(system, diagonal_step(system, bare))
    green_ref[0] = green[0]
    green_ref[1] = green[1]
    padded = tall.shape[2] // ORB
    for part in range(2):
        for lane in range(size // LANES):
            tall[part, lane, 0:size, :] = green[part][:, lane * LANES : (lane + 1) * LANES]
            tall[part, lane, size:, :] = jnp.zeros((padded * ORB - size, LANES), F32)
    rows = jnp.concatenate(
        [
            jnp.concatenate(
                [tall[part, lane, pl.ds(i, padded, stride=ORB), :] for lane in range(size // LANES)], axis=1
            )
            for part in range(2)
            for i in range(ORB)
        ],
        axis=0,
    )
    high, low = split(rows)
    mask = row_choice(pairs_ref, padded)
    for first in range(0, ORB, 2):
        choice = column_choice(pairs_ref, first, size)
        chosen = jnp.dot(high, choice, preferred_element_type=F32) + jnp.dot(
            low, choice, preferred_element_type=F32
        )
        total = jnp.sum(chosen.reshape(2 * ORB, padded, 2 * pairs) * mask[None], axis=1)
        for j in range(2):
            start = (first + j) * 2 * ORB
            blocks_ref[start : start + 2 * ORB, :] = total[:, j * pairs : (j + 1) * pairs]


def exchange_kernel(
    energies, momenta, shift_ref, occupation_ref, coupling_ref, blocks_ref, out_ref,
    weights, gathered, result, send_sem, recv_sem,
):
    devices = energies * momenta
    my_energy = lax.axis_index("energy")
    my_momentum = lax.axis_index("momentum")
    me = my_energy * momenta + my_momentum
    barrier = pltpu.get_barrier_semaphore()

    def peer(step):
        other = lax.rem(me + step, devices)
        return other, (other // momenta, lax.rem(other, momenta))

    def greet(step, carry):
        pl.semaphore_signal(barrier, inc=1, device_id=peer(step)[1], device_id_type=MESH)
        return carry

    lax.fori_loop(1, devices, greet, 0)
    pl.semaphore_wait(barrier, devices - 1)

    def send_blocks(step, carry):
        other, where = peer(step)
        pltpu.make_async_remote_copy(
            src_ref=blocks_ref.at[other], dst_ref=gathered.at[me],
            send_sem=send_sem.at[0], recv_sem=recv_sem.at[0],
            device_id=where, device_id_type=MESH,
        ).start()
        return carry

    lax.fori_loop(1, devices, send_blocks, 0)
    gathered[me] = blocks_ref[me]
    source = lax.broadcasted_iota(jnp.int32, (energies, 1, coupling_ref.shape[-1]), 0)
    couplings = [coupling_ref[m : m + 1, :][None] for m in range(coupling_ref.shape[0])]

    def weigh(target, carry):
        total = jnp.zeros(source.shape, F32)
        for m, strength in enumerate(couplings):
            level = occupation_ref[m]
            below = jnp.where(source == target - shift_ref[m], level, 0.0)
            above = jnp.where(source == target + shift_ref[m], level + 1.0, 0.0)
            total = total + (below + above) * strength
        weights[target] = total / momenta
        return carry

    lax.fori_loop(0, energies, weigh, 0)

    def all_of(buffer, semaphore):
        part = buffer.at[pl.ds(0, devices - 1)]
        pltpu.make_async_copy(part, part, semaphore).wait()

    all_of(blocks_ref, send_sem.at[0])
    all_of(gathered, recv_sem.at[0])
    sums = []
    for e in range(energies):
        total = gathered[e * momenta]
        for k in range(1, momenta):
            total = total + gathered[e * momenta + k]
        sums.append(total)

    def convolve(target, carry):
        total = sums[0] * weights[target, 0:1]
        for e in range(1, energies):
            total = total + sums[e] * weights[target, e : e + 1]
        result[target] = total
        return carry

    lax.fori_loop(0, energies, convolve, 0)

    def send_result(step, carry):
        other, where = peer(step)
        pltpu.make_async_remote_copy(
            src_ref=result.at[other // momenta], dst_ref=out_ref.at[me],
            send_sem=send_sem.at[1], recv_sem=recv_sem.at[1],
            device_id=where, device_id_type=MESH,
        ).start()
        return carry

    lax.fori_loop(1, devices, send_result, 0)
    out_ref[me] = result[my_energy]
    all_of(blocks_ref, send_sem.at[1])
    all_of(out_ref, recv_sem.at[1])


def final_kernel(system_ref, green_ref, blocks_ref, pairs_ref, out_ref, tall):
    size = system_ref.shape[-1]
    pairs = pairs_ref.shape[1]
    padded = tall.shape[2] // ORB
    mask = row_choice(pairs_ref, padded)
    spread = jnp.zeros((2 * ORB * padded, size), F32)
    for first in range(0, ORB, 2):
        start = first * 2 * ORB
        values = jnp.concatenate(
            [blocks_ref[start + j * 2 * ORB : start + (j + 1) * 2 * ORB, :] for j in range(2)], axis=1
        )
        wide = (values[:, None, :] * mask[None]).reshape(2 * ORB * padded, 2 * pairs)
        high, low = split(wide)
        choice = column_choice(pairs_ref, first, size)
        dims = (((1,), (1,)), ((), ()))
        spread = spread + lax.dot_general(high, choice, dims, preferred_element_type=F32)
        spread = spread + lax.dot_general(low, choice, dims, preferred_element_type=F32)
    for part in range(2):
        for i in range(ORB):
            start = (part * ORB + i) * padded
            for lane in range(size // LANES):
                tall[part, lane, pl.ds(i, padded, stride=ORB), :] = spread[
                    start : start + padded, lane * LANES : (lane + 1) * LANES
                ]
    system = tuple(
        system_ref[part]
        - jnp.concatenate([tall[part, lane, 0:size, :] for lane in range(size // LANES)], axis=1)
        for part in range(2)
    )
    final = newton(system, (green_ref[0], green_ref[1]))
    out_ref[0, 0, 0] = final[0]
    out_ref[0, 0, 1] = final[1]


def per_device(
    device_hamiltonian, lead_hamiltonian, lead_coupling, pair_atoms, phonon_shift, occupation, phonon_coupling
):
    energies = lax.axis_size("energy")
    momenta = lax.axis_size("momentum")
    devices = energies * momenta
    size = device_hamiltonian.shape[-1]
    pairs = pair_atoms.shape[1]
    entries = 2 * ORB * ORB
    share = -(-entries // devices)
    padded = 8 * (-(-size // (8 * ORB)))
    tall = pltpu.VMEM((2, size // LANES, padded * ORB, LANES), F32)
    params = functools.partial(pltpu.CompilerParams, vmem_limit_bytes=56 * 2**20)
    matrix = jax.ShapeDtypeStruct((2, size, size), F32)
    system, green, blocks = pl.pallas_call(
        functools.partial(first_kernel, energies),
        out_shape=(matrix, matrix, jax.ShapeDtypeStruct((entries, pairs), F32)),
        in_specs=[VMEM_SPEC] * 4,
        out_specs=(VMEM_SPEC,) * 3,
        scratch_shapes=[tall],
        compiler_params=params(),
        name="first_round",
    )(device_hamiltonian, lead_hamiltonian, lead_coupling, pair_atoms)
    blocks = jnp.pad(blocks, ((0, share * devices - entries), (0, 0))).reshape(devices, share, 1, pairs)
    received = pl.pallas_call(
        functools.partial(exchange_kernel, energies, momenta),
        out_shape=jax.ShapeDtypeStruct(blocks.shape, F32),
        in_specs=[SMEM_SPEC, SMEM_SPEC, VMEM_SPEC, VMEM_SPEC],
        out_specs=VMEM_SPEC,
        scratch_shapes=[
            pltpu.VMEM((energies, energies, 1, pairs), F32),
            pltpu.VMEM(blocks.shape, F32),
            pltpu.VMEM((energies,) + blocks.shape[1:], F32),
            pltpu.SemaphoreType.DMA((2,)),
            pltpu.SemaphoreType.DMA((2,)),
        ],
        compiler_params=params(collective_id=0, has_side_effects=True),
        name="exchange",
    )(phonon_shift, occupation, phonon_coupling, blocks)
    received = received.reshape(devices * share, pairs)[:entries]
    return pl.pallas_call(
        final_kernel,
        out_shape=jax.ShapeDtypeStruct((1, 1, 2, size, size), F32),
        in_specs=[VMEM_SPEC] * 4,
        out_specs=VMEM_SPEC,
        scratch_shapes=[tall],
        compiler_params=params(),
        name="final_round",
    )(system, green, received, pair_atoms)


def solution(mesh):
    matrices = P("momentum", None, None, None)
    return jax.shard_map(
        per_device,
        mesh=mesh,
        in_specs=(matrices, matrices, matrices, P(), P(), P(), P()),
        out_specs=P("energy", "momentum", None, None, None),
        check_vma=False,
    )
```

```python
import functools

import jax
import jax.numpy as jnp
from jax import lax
from jax.experimental import pallas as pl
from jax.experimental.pallas import tpu as pltpu
from jax.sharding import PartitionSpec as P

ORB = 12
NEWTON = 2
LANES = 128
F32 = jnp.float32
BF16 = jnp.bfloat16
MESH = pl.DeviceIdType.MESH
VMEM_SPEC = pl.BlockSpec(memory_space=pltpu.VMEM)
SMEM_SPEC = pl.BlockSpec(memory_space=pltpu.SMEM)


def split(value):
    high = value.astype(BF16)
    return high, (value - high.astype(F32)).astype(BF16)


def prepare(matrix):
    real, imag = matrix
    return split(real), split(imag), split(real + imag)


def real_product(left, right, transposed):
    dims = (((1,), (1 if transposed else 0,)), ((), ()))
    dot = functools.partial(lax.dot_general, dimension_numbers=dims, preferred_element_type=F32)
    return dot(left[0], right[0]) + (dot(left[0], right[1]) + dot(left[1], right[0]))


def complex_product(left, right, transposed=False):
    reals = real_product(left[0], right[0], transposed)
    imags = real_product(left[1], right[1], transposed)
    mixed = real_product(left[2], right[2], transposed)
    return reals - imags, mixed - reals - imags


def identity_mask(size):
    rows = lax.broadcasted_iota(jnp.int32, (size, size), 0)
    return rows == lax.broadcasted_iota(jnp.int32, (size, size), 1)


def inverse(real, imag):
    modulus = real * real + imag * imag
    return real / modulus, -imag / modulus


def diagonal_step(system, bare):
    eye = identity_mask(system[0].shape[0])
    masked = [jnp.where(eye, part, 0.0) for part in bare]
    row_real, row_imag = inverse(*[jnp.sum(part, axis=0, keepdims=True) for part in masked])
    col_real, col_imag = inverse(*[jnp.sum(part, axis=1, keepdims=True) for part in masked])
    step_real = system[0] * row_real - system[1] * row_imag
    step_imag = system[0] * row_imag + system[1] * row_real
    both_real = col_real * step_real - col_imag * step_imag
    both_imag = col_real * step_imag + col_imag * step_real
    return (
        jnp.where(eye, 2.0 * row_real, 0.0) - both_real,
        jnp.where(eye, 2.0 * row_imag, 0.0) - both_imag,
    )


def newton(system, current):
    factor = prepare(system)
    for _ in range(NEWTON):
        held = prepare(current)
        residual = complex_product(factor, held)
        change = complex_product(held, prepare(residual))
        current = (2.0 * current[0] - change[0], 2.0 * current[1] - change[1])
    return current


def column_choice(pairs_ref, first, size):
    columns = lax.broadcasted_iota(jnp.int32, (size, pairs_ref.shape[1]), 0)
    starts = ORB * pairs_ref[1:2, :]
    picks = [(columns == starts + (first + j)).astype(F32).astype(BF16) for j in range(2)]
    return jnp.concatenate(picks, axis=1)


def row_choice(pairs_ref, atoms_padded):
    atoms = lax.broadcasted_iota(jnp.int32, (atoms_padded, pairs_ref.shape[1]), 0)
    mask = (atoms == pairs_ref[0:1, :]).astype(F32)
    return jnp.concatenate([mask, mask], axis=1)


def first_kernel(energies, dh_ref, lh_ref, lc_ref, pairs_ref, system_ref, green_ref, blocks_ref, tall):
    size = dh_ref.shape[-1]
    pairs = pairs_ref.shape[1]
    energy = -1.0 + 2.0 * (lax.axis_index("energy").astype(F32) + 0.5) / energies
    eye = identity_mask(size)
    shift = jnp.where(eye, energy, 0.0)
    lead = (shift - lh_ref[0, 0], -lh_ref[0, 1])
    green_lead = newton(lead, diagonal_step(lead, lead))
    coupling = prepare((lc_ref[0, 0], lc_ref[0, 1]))
    contact = complex_product(
        prepare(complex_product(coupling, prepare(green_lead))), coupling, transposed=True
    )
    bare = (shift - dh_ref[0, 0], -dh_ref[0, 1])
    system = (bare[0] - contact[0], bare[1] - contact[1])
    system_ref[0] = system[0]
    system_ref[1] = system[1]
    green = newton(system, diagonal_step(system, bare))
    green_ref[0] = green[0]
    green_ref[1] = green[1]
    padded = tall.shape[2] // ORB
    for part in range(2):
        for lane in range(size // LANES):
            tall[part, lane, 0:size, :] = green[part][:, lane * LANES : (lane + 1) * LANES]
            tall[part, lane, size:, :] = jnp.zeros((padded * ORB - size, LANES), F32)
    rows = jnp.concatenate(
        [
            jnp.concatenate(
                [tall[part, lane, pl.ds(i, padded, stride=ORB), :] for lane in range(size // LANES)], axis=1
            )
            for part in range(2)
            for i in range(ORB)
        ],
        axis=0,
    )
    high, low = split(rows)
    mask = row_choice(pairs_ref, padded)
    for first in range(0, ORB, 2):
        choice = column_choice(pairs_ref, first, size)
        chosen = jnp.dot(high, choice, preferred_element_type=F32) + jnp.dot(
            low, choice, preferred_element_type=F32
        )
        total = jnp.sum(chosen.reshape(2 * ORB, padded, 2 * pairs) * mask[None], axis=1)
        for j in range(2):
            start = (first + j) * 2 * ORB
            blocks_ref[start : start + 2 * ORB, :] = total[:, j * pairs : (j + 1) * pairs]


def each(count, body):
    if count <= 16:
        for step in range(1, count):
            body(step)
    else:
        lax.fori_loop(1, count, lambda step, carry: (body(step), carry)[1], 0)


def exchange_kernel(
    energies, momenta, shift_ref, occupation_ref, coupling_ref, blocks_ref, out_ref,
    weights, partner_half, half, gathered, result, send_sem, recv_sem,
):
    halves, groups = blocks_ref.shape[:2]
    columns = momenta // halves
    my_energy = lax.axis_index("energy")
    my_momentum = lax.axis_index("momentum")
    my_column = my_momentum // halves
    my_half = lax.rem(my_momentum, halves)
    me = my_energy * columns + my_column
    other_half = halves - 1 - my_half
    partner = (my_energy, my_column * halves + other_half)
    barrier = pltpu.get_barrier_semaphore()

    def peer(step):
        other = lax.rem(me + step, groups)
        return other, (other // columns, lax.rem(other, columns) * halves + my_half)

    def send(source, target, phase, where):
        return pltpu.make_async_remote_copy(
            src_ref=source, dst_ref=target, send_sem=send_sem.at[phase], recv_sem=recv_sem.at[phase],
            device_id=where, device_id_type=MESH,
        )

    def greet(where):
        pl.semaphore_signal(barrier, inc=1, device_id=where, device_id_type=MESH)

    if halves > 1:
        greet(partner)
    each(groups, lambda step: greet(peer(step)[1]))
    source = lax.broadcasted_iota(jnp.int32, (energies, 1, coupling_ref.shape[-1]), 0)
    couplings = [coupling_ref[m : m + 1, :][None] for m in range(coupling_ref.shape[0])]

    def weigh(target, carry):
        total = jnp.zeros(source.shape, F32)
        for m, strength in enumerate(couplings):
            level = occupation_ref[m]
            below = jnp.where(source == target - shift_ref[m], level, 0.0)
            above = jnp.where(source == target + shift_ref[m], level + 1.0, 0.0)
            total = total + (below + above) * strength
        weights[target] = total / momenta
        return carry

    lax.fori_loop(0, energies, weigh, 0)
    pl.semaphore_wait(barrier, groups - 1 + halves - 1)

    if halves > 1:
        swap = send(blocks_ref.at[other_half], partner_half, 0, partner)
        swap.start()
        swap.wait()
        half[...] = blocks_ref[my_half] + partner_half[...]
    else:
        half[...] = blocks_ref[0]

    def send_blocks(step):
        other, where = peer(step)
        send(half.at[other], gathered.at[me], 1, where).start()

    each(groups, send_blocks)
    gathered[me] = half[me]

    def all_of(buffer, semaphore):
        part = buffer.at[pl.ds(0, groups - 1)]
        pltpu.make_async_copy(part, part, semaphore).wait()

    all_of(gathered, recv_sem.at[1])
    sums = []
    for e in range(energies):
        total = gathered[e * columns]
        for k in range(1, columns):
            total = total + gathered[e * columns + k]
        sums.append(total)

    def convolve(target):
        total = sums[0] * weights[target, 0:1]
        for e in range(1, energies):
            total = total + sums[e] * weights[target, e : e + 1]
        result[target] = total

    def send_result(step):
        target = lax.rem(my_energy + step, energies)
        convolve(target)
        for k in range(columns):
            where = (target, k * halves + my_half)
            send(result.at[target], out_ref.at[my_half, me], 2, where).start()

    each(energies, send_result)
    convolve(my_energy)
    for k in range(1, columns):
        where = (my_energy, lax.rem(my_column + k, columns) * halves + my_half)
        send(result.at[my_energy], out_ref.at[my_half, me], 2, where).start()
    out_ref[my_half, me] = result[my_energy]
    all_of(out_ref.at[0], recv_sem.at[2])
    if halves > 1:
        share = send(out_ref.at[my_half], out_ref.at[my_half], 3, partner)
        share.start()
        share.wait()
    all_of(half, send_sem.at[1])
    all_of(half, send_sem.at[2])


def final_kernel(system_ref, green_ref, blocks_ref, pairs_ref, out_ref, tall):
    size = system_ref.shape[-1]
    pairs = pairs_ref.shape[1]
    padded = tall.shape[2] // ORB
    mask = row_choice(pairs_ref, padded)
    spread = jnp.zeros((2 * ORB * padded, size), F32)
    for first in range(0, ORB, 2):
        start = first * 2 * ORB
        values = jnp.concatenate(
            [blocks_ref[start + j * 2 * ORB : start + (j + 1) * 2 * ORB, :] for j in range(2)], axis=1
        )
        wide = (values[:, None, :] * mask[None]).reshape(2 * ORB * padded, 2 * pairs)
        high, low = split(wide)
        choice = column_choice(pairs_ref, first, size)
        dims = (((1,), (1,)), ((), ()))
        spread = spread + lax.dot_general(high, choice, dims, preferred_element_type=F32)
        spread = spread + lax.dot_general(low, choice, dims, preferred_element_type=F32)
    for part in range(2):
        for i in range(ORB):
            start = (part * ORB + i) * padded
            for lane in range(size // LANES):
                tall[part, lane, pl.ds(i, padded, stride=ORB), :] = spread[
                    start : start + padded, lane * LANES : (lane + 1) * LANES
                ]
    system = tuple(
        system_ref[part]
        - jnp.concatenate([tall[part, lane, 0:size, :] for lane in range(size // LANES)], axis=1)
        for part in range(2)
    )
    final = newton(system, (green_ref[0], green_ref[1]))
    out_ref[0, 0, 0] = final[0]
    out_ref[0, 0, 1] = final[1]


def per_device(
    device_hamiltonian, lead_hamiltonian, lead_coupling, pair_atoms, phonon_shift, occupation, phonon_coupling
):
    energies = lax.axis_size("energy")
    momenta = lax.axis_size("momentum")
    halves = 2 if momenta % 2 == 0 else 1
    groups = energies * momenta // halves
    size = device_hamiltonian.shape[-1]
    pairs = pair_atoms.shape[1]
    entries = 2 * ORB * ORB
    share = -(-entries // (halves * groups))
    padded = 8 * (-(-size // (8 * ORB)))
    tall = pltpu.VMEM((2, size // LANES, padded * ORB, LANES), F32)
    params = functools.partial(pltpu.CompilerParams, vmem_limit_bytes=56 * 2**20)
    matrix = jax.ShapeDtypeStruct((2, size, size), F32)
    system, green, blocks = pl.pallas_call(
        functools.partial(first_kernel, energies),
        out_shape=(matrix, matrix, jax.ShapeDtypeStruct((entries, pairs), F32)),
        in_specs=[VMEM_SPEC] * 4,
        out_specs=(VMEM_SPEC,) * 3,
        scratch_shapes=[tall],
        compiler_params=params(),
        name="first_round",
    )(device_hamiltonian, lead_hamiltonian, lead_coupling, pair_atoms)
    filled = halves * groups * share
    blocks = jnp.pad(blocks, ((0, filled - entries), (0, 0))).reshape(halves, groups, share, 1, pairs)
    received = pl.pallas_call(
        functools.partial(exchange_kernel, energies, momenta),
        out_shape=jax.ShapeDtypeStruct(blocks.shape, F32),
        in_specs=[SMEM_SPEC, SMEM_SPEC, VMEM_SPEC, VMEM_SPEC],
        out_specs=VMEM_SPEC,
        scratch_shapes=[
            pltpu.VMEM((energies, energies, 1, pairs), F32),
            pltpu.VMEM(blocks.shape[1:], F32),
            pltpu.VMEM(blocks.shape[1:], F32),
            pltpu.VMEM(blocks.shape[1:], F32),
            pltpu.VMEM((energies,) + blocks.shape[2:], F32),
            pltpu.SemaphoreType.DMA((4,)),
            pltpu.SemaphoreType.DMA((4,)),
        ],
        compiler_params=params(collective_id=0, has_side_effects=True),
        name="exchange",
    )(phonon_shift, occupation, phonon_coupling, blocks)
    received = received.reshape(filled, pairs)[:entries]
    return pl.pallas_call(
        final_kernel,
        out_shape=jax.ShapeDtypeStruct((1, 1, 2, size, size), F32),
        in_specs=[VMEM_SPEC] * 4,
        out_specs=VMEM_SPEC,
        scratch_shapes=[tall],
        compiler_params=params(),
        name="final_round",
    )(system, green, received, pair_atoms)


def solution(mesh):
    matrices = P("momentum", None, None, None)
    return jax.shard_map(
        per_device,
        mesh=mesh,
        in_specs=(matrices, matrices, matrices, P(), P(), P(), P()),
        out_specs=P("energy", "momentum", None, None, None),
        check_vma=False,
    )
```
